32 devices in a mesh: row: 4 (over y, x), col: 4 (over z), dp: 2 (over core).
Axes of the slice: x: 2, y: 2, z: 4, core: 2. Of those that a mesh axis runs over, the one named last changes fastest.
Arguments:
- inputs: bfloat16 [1024, 8192], P(('col', 'dp'), 'row'), may hold values from -6 to 6
- gate_weight: bfloat16 [8192, 14336], P('row', 'col'), may hold values from -0.0625 to 0.0625
- up_weight: bfloat16 [8192, 14336], P('row', 'col'), may hold values from -0.0625 to 0.0625
- down_weight: bfloat16 [14336, 8192], P('col', 'row'), may hold values from -0.046875 to 0.046875
- reward_head: bfloat16 [8192], P('row'), may hold values from -0.0625 to 0.0625
- upstream: bfloat16 [1024, 8192], P(('col', 'dp'), 'row'), may hold values from -0.59765625 to 0.59765625
- labels: int32 [1024], P(('col', 'dp')), may hold values from 0 to 1
- label_mask: int32 [1024], P(('col', 'dp')), may hold values 0 or 1
Outputs:
- gate_grad: float32 [8192, 14336], P(('row', 'dp'), 'col')
- up_grad: float32 [8192, 14336], P(('row', 'dp'), 'col')
- down_grad: float32 [14336, 8192], P(('col', 'dp'), 'row')
- input_grad: float32 [1024, 8192], P(('col', 'dp'), 'row')
The draws below stay inside these ranges and needn't reach their ends.
All inputs are finite; a program needn't handle non-finite values. No bound on the sum of `label_mask` on one device may be relied on, other than what follows from the above.
Results may differ from the reference program's by a relative error of at most 0.035.
Values may be sent and summed in bfloat16 or wider, within the bound.
A program may use at most 192 MiB of HBM per device.

```python
import jax
import jax.numpy as jnp
from jax import lax

D = 8192
FF = 14336
TOK_DEV = 128
TOKENS = 1024
N_ROW = 4
N_COL = 4
N_DP = 2


def set_ends(entries, key, low, high):
    spot = [jax.random.randint(jax.random.fold_in(key, axis), (), 0, length) for axis, length in enumerate(entries.shape)]
    main_axis = entries.shape.index(max(entries.shape))
    beside = spot[:main_axis] + [(spot[main_axis] + 1) % entries.shape[main_axis]] + spot[main_axis + 1:]
    return entries.at[tuple(spot)].set(low).at[tuple(beside)].set(high)


def level_of(rng, dims, shards, low, high):
    def one(position, shards_of):
        steps = jax.random.uniform(jax.random.fold_in(jax.random.fold_in(rng, 6), position), (shards_of,), jnp.float32, low / len(shards), high / len(shards))
        return jnp.repeat(jnp.exp(steps), dims[position] // shards_of).reshape((-1,) + (1,) * (len(dims) - position - 1))

    factor_of = one(*shards[0])
    for cut in shards[1:]:
        factor_of = factor_of * one(*cut)
    return factor_of


def scatter_about(key, dims, deviation, limit, cuts=(), held_as=jnp.bfloat16):
    result = deviation * jax.random.normal(key, dims, jnp.float32)
    if cuts:
        result = result * level_of(key, dims, cuts, -0.22, 0.18)
    return jnp.clip(result, -limit, limit).astype(held_as)


def setup_inputs(seed: int = 0) -> dict:
    splits = jax.random.split(jax.random.key(seed), 9)
    inputs = scatter_about(splits[0], (TOKENS, D), 1.0, 6.0, ((0, 8), (1, 4)))
    gate_weight = scatter_about(splits[1], (D, FF), D ** -0.5, 0.0625, ((0, 4), (1, 4)))
    up_weight = scatter_about(splits[2], (D, FF), D ** -0.5, 0.0625, ((0, 4), (1, 4)))
    down_weight = scatter_about(splits[3], (FF, D), FF ** -0.5, 0.046875, ((0, 4), (1, 4)))
    reward_head = scatter_about(splits[4], (D,), D ** -0.5, 0.0625, ((0, 4),))
    upstream = scatter_about(splits[5], (TOKENS, D), 0.1, 0.59765625, ((0, 8), (1, 4)))
    labels = set_ends(jax.random.randint(splits[6], (TOKENS,), 0, 2), jax.random.fold_in(splits[6], 1), 0, 1).astype(jnp.int32)
    label_mask = set_ends((jax.random.randint(splits[7], (TOKENS,), 0, 2) < 1).astype(jnp.int32), jax.random.fold_in(splits[7], 1), 0, 1)
    return dict(inputs=inputs, gate_weight=gate_weight, up_weight=up_weight, down_weight=down_weight, reward_head=reward_head, upstream=upstream, labels=labels, label_mask=label_mask)


def rounded(value):
    return lax.optimization_barrier(value.astype(jnp.bfloat16)).astype(jnp.float32)


def transpose_product(left, right):
    return lax.dot_general(left, right, (((0,), (0,)), ((), ())), preferred_element_type=jnp.float32)


def right_transpose(left, right):
    return lax.dot_general(left, right, (((1,), (1,)), ((), ())), preferred_element_type=jnp.float32)


def replica_rows(array, replica):
    return array.reshape(N_COL, N_DP, TOK_DEV, array.shape[-1])[:, replica].reshape(-1, array.shape[-1])


def reference(inputs, gate_weight, up_weight, down_weight, reward_head, upstream, labels, label_mask):
    span = D // N_ROW
    gate = jnp.zeros((TOKENS, FF), jnp.float32)
    upper = jnp.zeros((TOKENS, FF), jnp.float32)
    for block in range(N_ROW):
        cols = inputs[:, block * span:(block + 1) * span]
        gate = gate + rounded(jnp.dot(cols, gate_weight[block * span:(block + 1) * span], preferred_element_type=jnp.float32))
        upper = upper + rounded(jnp.dot(cols, up_weight[block * span:(block + 1) * span], preferred_element_type=jnp.float32))
    sig = jax.nn.sigmoid(gate)
    hidden = (gate * sig * upper).astype(jnp.bfloat16)
    outcome = inputs.astype(jnp.float32) + jnp.dot(hidden, down_weight, preferred_element_type=jnp.float32)
    head_value = reward_head.astype(jnp.float32)
    score = jnp.dot(outcome, head_value, precision=lax.Precision.HIGHEST)
    slope = 8.0 * label_mask.astype(jnp.float32) * (jax.nn.sigmoid(score) - labels.astype(jnp.float32))
    grad_out = upstream.astype(jnp.float32) + slope[:, None] * head_value[None, :]
    grad_mixed = grad_out.astype(jnp.bfloat16)
    grad_hidden = right_transpose(grad_mixed, down_weight)
    grad_gate = (grad_hidden * upper * sig * (1.0 + gate * (1.0 - sig))).astype(jnp.bfloat16)
    grad_upper = (grad_hidden * gate * sig).astype(jnp.bfloat16)
    input_grad = grad_out + right_transpose(grad_gate, gate_weight) + right_transpose(grad_upper, up_weight)
    gate_grad = jnp.zeros((D, FF), jnp.float32)
    up_grad = jnp.zeros((D, FF), jnp.float32)
    down_grad = jnp.zeros((FF, D), jnp.float32)
    for replica in range(N_DP):
        x_part = replica_rows(inputs, replica)
        gate_grad = gate_grad + rounded(transpose_product(x_part, replica_rows(grad_gate, replica)))
        up_grad = up_grad + rounded(transpose_product(x_part, replica_rows(grad_upper, replica)))
        down_grad = down_grad + rounded(transpose_product(replica_rows(hidden, replica), replica_rows(grad_mixed, replica)))
    return gate_grad, up_grad, down_grad, input_grad
```

```python
import jax
import jax.numpy as jnp
from jax import lax
from jax.sharding import PartitionSpec as P

reward_weight = 8.0
CHUNKS = 2
F32 = jnp.float32
BF16 = jnp.bfloat16


def transpose_product(left, right):
    return lax.dot_general(left, right, (((0,), (0,)), ((), ())), preferred_element_type=F32)


def right_transpose(left, right):
    return lax.dot_general(left, right, (((1,), (1,)), ((), ())), preferred_element_type=F32)


def swap(value, axis, distance):
    size = lax.axis_size(axis)
    return lax.ppermute(value, axis, [(i, i ^ distance) for i in range(size)])


def bit_orders():
    bits = (lax.axis_size("row") - 1).bit_length()
    return list(range(bits)), list(reversed(range(bits)))


def row_scatter(value, order):
    size = lax.axis_size("row")
    me = lax.axis_index("row")
    bits = (size - 1).bit_length()
    count = value.shape[0] // size
    total = value.reshape((2,) * bits + (count, value.shape[1]))
    left = list(reversed(range(bits)))
    for bit in order:
        axis = left.index(bit)
        left.remove(bit)
        mine = (me >> bit) & 1
        keep = lax.dynamic_index_in_dim(total, mine, axis, keepdims=False)
        send = lax.dynamic_index_in_dim(total, 1 - mine, axis, keepdims=False)
        total = keep.astype(F32) + swap(send.astype(BF16), "row", 1 << bit).astype(F32)
    return total


def row_gather(value, order):
    size = lax.axis_size("row")
    me = lax.axis_index("row")
    bits = (size - 1).bit_length()
    held = value
    left = []
    for bit in order:
        axis = len([b for b in left if b > bit])
        other = swap(held, "row", 1 << bit)
        mine = (me >> bit) & 1
        low = jnp.where(mine == 0, held, other)
        high = jnp.where(mine == 0, other, held)
        held = jnp.stack([low, high], axis=axis)
        left = sorted(left + [bit], reverse=True)
    return held.reshape((size * value.shape[0],) + value.shape[1:])


def row_sum(value):
    total = value
    for distance in range(1, lax.axis_size("row")):
        total = total + swap(value, "row", distance)
    return total


def col_gather(value):
    size = lax.axis_size("col")
    me = lax.axis_index("col")
    up, down = [value], [value]
    for step in range(1, size):
        up.append(lax.ppermute(up[-1], "col", [(i, i + 1) for i in range(step - 1, size - 1)]))
        down.append(lax.ppermute(down[-1], "col", [(i, i - 1) for i in range(1, size - step + 1)]))
    blocks = [value]
    for k in range(1, size):
        blocks.append(jnp.where(me >= k, up[k], down[size - k]))
    return jnp.concatenate(blocks, axis=0)


def col_scatter(value):
    size = lax.axis_size("col")
    blocks = jnp.split(value, size, axis=0)
    up, down = blocks[1], blocks[size - 1]
    for step in range(1, size):
        if step > 1:
            up = (up.astype(F32) + blocks[step].astype(F32)).astype(BF16)
            down = (down.astype(F32) + blocks[size - step].astype(F32)).astype(BF16)
        up = lax.ppermute(up, "col", [(i, i + 1) for i in range(step)])
        down = lax.ppermute(down, "col", [(i, i - 1) for i in range(size - step, size)])
    return blocks[0].astype(F32) + (up.astype(F32) + down.astype(F32))


def with_peer_half(value, axis_halves):
    d = lax.axis_index("dp")
    half = value.shape[1] // axis_halves
    mine = lax.dynamic_slice_in_dim(value, d * half, half, axis=1)
    send = lax.dynamic_slice_in_dim(value, (1 - d) * half, half, axis=1)
    return jnp.concatenate([mine, swap(send, "dp", 1)], axis=0)


def with_peer(value):
    return jnp.concatenate([value, swap(value, "dp", 1)], axis=0)


def per_device(
    inputs, gate_weight, up_weight, down_weight, reward_head, upstream, labels, label_mask
):
    head_value = reward_head.astype(F32)
    low_first, high_first = bit_orders()
    count = inputs.shape[0] // CHUNKS
    middle = gate_weight.shape[1] // 2

    def part(array, c):
        return array[c * count:(c + 1) * count]

    gathered = [col_gather(part(inputs, c)) for c in range(CHUNKS)]
    gate_grad = up_grad = down_grad = None
    input_grads = []
    for c in range(CHUNKS):
        rows = gathered[c]
        gate = row_scatter(
            jnp.dot(rows, gate_weight, preferred_element_type=F32).astype(BF16), low_first
        )
        upper = row_scatter(
            jnp.dot(rows, up_weight, preferred_element_type=F32).astype(BF16), high_first
        )
        sigmoid_gate = jax.nn.sigmoid(gate)
        hidden = (gate * sigmoid_gate * upper).astype(BF16)
        hidden_all = jnp.concatenate(
            [
                row_gather(hidden[:, :middle], low_first),
                row_gather(hidden[:, middle:], high_first),
            ],
            axis=1,
        )
        mixed = col_scatter(
            jnp.dot(hidden_all, down_weight, preferred_element_type=F32).astype(BF16)
        )
        outcome = part(inputs, c).astype(F32) + mixed
        score = row_sum(jnp.sum(outcome * head_value[None, :], axis=1))
        slope = (
            reward_weight
            * part(label_mask, c).astype(F32)
            * (jax.nn.sigmoid(score) - part(labels, c).astype(F32))
        )
        grad_out = part(upstream, c).astype(F32) + slope[:, None] * head_value[None, :]
        grad_rows = col_gather(grad_out.astype(BF16))
        product = right_transpose(grad_rows, down_weight).astype(BF16)
        grad_hidden = jnp.concatenate(
            [
                row_scatter(product[:, :middle], low_first),
                row_scatter(product[:, middle:], high_first),
            ],
            axis=1,
        )
        grad_gate = (
            grad_hidden * upper * sigmoid_gate * (1.0 + gate * (1.0 - sigmoid_gate))
        ).astype(BF16)
        grad_upper = (grad_hidden * gate * sigmoid_gate).astype(BF16)
        gate_all = row_gather(grad_gate, low_first)
        upper_all = row_gather(grad_upper, high_first)
        input_term = right_transpose(gate_all, gate_weight) + right_transpose(upper_all, up_weight)
        input_grads.append(grad_out + col_scatter(input_term.astype(BF16)))

        rows_both = with_peer_half(rows, 2)
        down_c = transpose_product(with_peer_half(hidden_all, 2), with_peer(grad_rows))
        gate_c = transpose_product(rows_both, with_peer(gate_all))
        up_c = transpose_product(rows_both, with_peer(upper_all))
        down_grad = down_c if down_grad is None else down_grad + down_c
        gate_grad = gate_c if gate_grad is None else gate_grad + gate_c
        up_grad = up_c if up_grad is None else up_grad + up_c
    return (gate_grad, up_grad, down_grad, jnp.concatenate(input_grads, axis=0))


def solution(mesh):
    in_specs = (
        P(("col", "dp"), "row"),
        P("row", "col"),
        P("row", "col"),
        P("col", "row"),
        P("row"),
        P(("col", "dp"), "row"),
        P(("col", "dp")),
        P(("col", "dp")),
    )
    out_specs = (
        P(("row", "dp"), "col"),
        P(("row", "dp"), "col"),
        P(("col", "dp"), "row"),
        P(("col", "dp"), "row"),
    )
    return jax.shard_map(
        per_device, mesh=mesh, in_specs=in_specs, out_specs=out_specs, check_vma=False
    )
```
